128 devices in a mesh: rows: 4 (over x_hi, core), cols: 8 (over y, x_lo), depth: 4 (over z).
Axes of the slice: x: 4 (x_hi: 2, x_lo: 2; x = x_hi * 2 + x_lo), y: 4, z: 4, core: 2. Of those that a mesh axis runs over, the one named last changes fastest.
Arguments:
- left_factor: bfloat16 [5000, 4096], P('rows', ('cols', 'depth')), may hold values from -0.71875 to 0.71875
- right_factor: bfloat16 [5000, 4, 4096], P('rows', 'depth', 'cols'), may hold values from -0.71875 to 0.71875
- amplitudes: bfloat16 [4096, 4, 2048], P('rows', 'depth'), may hold values from -0.119628906 to 0.119628906
- pair_list: int32 [4096, 2], P(('rows', 'depth')), may hold values from 0 to 119, as said below
- offsets: int32 [2], replicated, may hold values from 0 to 1272
- occ_energy: float32 [120], replicated, may hold values from -1.5 to -0.5
- virt_energy: float32 [1400], replicated, may hold values from 0.2 to 1.5
Outputs:
- update: float32 [4096, 8192], P(('rows', 'depth'), 'cols')
The draws below stay inside these ranges and needn't reach their ends.
Inputs may be any that keep to these rules, and one draw needn't show every extreme that they name: `pair_list`: each row is a pair i <= j of occupied orbitals, no pair occurs twice, and the pair (0, 119) is always present.
All inputs are finite; a program needn't handle non-finite values.
Results may differ from the reference program's by a relative error of at most 0.0029.
Values may be sent and summed in bfloat16 or wider, within the bound.
No kernel may reach another device: no remote copies, remote signals or barrier semaphores. Data moves between devices by JAX's collectives and lax.ppermute only.
A program may use at most 64 MiB of HBM per device.

```python
import jax
import jax.numpy as jnp
from jax import lax

NOCC = 120
NVIRT = 1400
NAUX = 5000
A = 64
B = 128
C = 64
D = 128
PAIRS = 4096
DL = 32


def draw_pair_list(key, part):
    key = jax.random.fold_in(key, 11)
    total = NOCC * (NOCC + 1) // 2
    scores = jax.random.randint(key, (total,), 0, 1 << 16) * total + jnp.arange(total, dtype=jnp.int32)
    scores = scores.at[NOCC - 1].set(-1)
    chosen = jnp.argsort(scores)[:PAIRS].astype(jnp.int32)
    levels = jnp.arange(NOCC, dtype=jnp.int32)
    starts = levels * NOCC - levels * (levels - 1) // 2
    first = jnp.sum((starts[None, 1:] <= chosen[:, None]).astype(jnp.int32), axis=1)
    second = first + chosen - starts[first]
    return jnp.stack([first, second], 1).astype(jnp.int32)


def shard_levels(key, shape, split, low, top_value):
    def one(axis_at, blocks):
        heights = jax.random.uniform(jax.random.fold_in(jax.random.fold_in(key, 6), axis_at), (blocks,), jnp.float32, low / len(split), top_value / len(split))
        return jnp.repeat(jnp.exp(heights), shape[axis_at] // blocks).reshape((-1,) + (1,) * (len(shape) - axis_at - 1))

    gain = one(*split[0])
    for cut in split[1:]:
        gain = gain * one(*cut)
    return gain


def scatter_about(stream_key, dims, deviation, bound, pieces=(), held_as=jnp.bfloat16):
    level = shard_levels(stream_key, dims, pieces, -0.22, 0.18) if pieces else 1.0
    result = jax.random.normal(stream_key, dims, jnp.float32) * deviation * level
    return jnp.minimum(jnp.maximum(result, -bound), bound).astype(held_as)


def setup_inputs(seed: int = 0) -> dict:
    key_of = jax.random.split(jax.random.key(seed), 8)
    return {
        "left_factor": scatter_about(key_of[0], (NAUX, A * C), 0.12, 0.71875, ((0, 4), (1, 32))),
        "right_factor": scatter_about(key_of[1], (NAUX, D // DL, B * DL), 0.12, 0.71875, ((0, 4), (1, 4), (2, 8))),
        "amplitudes": scatter_about(key_of[2], (PAIRS, D // DL, C * DL), 0.02, 0.119628906, ((0, 4), (1, 4))),
        "pair_list": draw_pair_list(jax.random.fold_in(key_of[7], 71), 0),
        "offsets": jax.random.randint(key_of[4], (2,), 0, NVIRT - B + 1).astype(jnp.int32),
        "occ_energy": jnp.clip(jax.random.uniform(key_of[5], (NOCC,), jnp.float32, -1.5, -0.5), -1.5, -0.5),
        "virt_energy": jnp.clip(jax.random.uniform(key_of[6], (NVIRT,), jnp.float32, 0.2, 1.5), 0.2, 1.5),
    }


def reference(left_factor, right_factor, amplitudes, pair_list, offsets, occ_energy, virt_energy):
    blocks = D // DL
    right_rows = right_factor.reshape(NAUX, blocks, B, DL).transpose(0, 2, 1, 3).reshape(NAUX, B * D)
    integrals = lax.dot_general(left_factor, right_rows, (((0,), (0,)), ((), ())), preferred_element_type=jnp.float32).astype(jnp.bfloat16)
    integrals = integrals.reshape(A, C, B, D).transpose(1, 3, 2, 0).reshape(C * D, B * A)
    amp_rows = amplitudes.reshape(PAIRS, blocks, C, DL).transpose(0, 2, 1, 3).reshape(PAIRS, C * D)
    ladder = jnp.dot(amp_rows, integrals, preferred_element_type=jnp.float32).reshape(PAIRS, B, A)
    energy_a = lax.dynamic_slice(virt_energy, (offsets[0],), (A,))
    energy_b = lax.dynamic_slice(virt_energy, (offsets[1],), (B,))
    first = pair_list[:, 0]
    second = pair_list[:, 1]
    occupied = occ_energy[first] + occ_energy[second]
    weight = jnp.where(first == second, 0.5, 1.0).astype(occ_energy.dtype)
    denominator = energy_b[None, :, None] + energy_a[None, None, :] - occupied[:, None, None]
    return (ladder * weight[:, None, None] / denominator).reshape(PAIRS, B * A)
```

```python
import functools

import jax
import jax.numpy as jnp
import numpy as np
from jax import lax
from jax.experimental import pallas as pl
from jax.experimental.pallas import tpu as pltpu
from jax.sharding import PartitionSpec as P

A = 64
B = 128
C = 64
DL = 32
CHUNKS = 2
AXES = ("rows", "cols", "depth")
VMEM = pl.BlockSpec(memory_space=pltpu.VMEM)
SMEM = pl.BlockSpec(memory_space=pltpu.SMEM)
MIB = 1 << 20


def swap_table(xh=0, core=0, y=0, xl=0, z=0):
    table = []
    for i in range(128):
        rows, cols, depth = i // 32, (i // 4) % 8, i % 4
        rows ^= xh * 2 + core
        cols ^= y * 2 + xl
        table.append((i, rows * 32 + cols * 4 + (depth ^ z)))
    return table


def swap(x, **by):
    return lax.ppermute(x, AXES, swap_table(**by))


def dot_nt(u, v):
    return lax.dot_general(u, v, (((1,), (1,)), ((), ())), preferred_element_type=jnp.float32)


def tile_kernel(*refs):
    z, la, lb, r = refs[0], refs[1:5], refs[5:9], refs[9:17]
    keep, send = refs[17:19]
    acc = refs[19]
    r_own = jnp.concatenate([r[0][...], r[1][...], r[4][...], r[5][...]], axis=1)
    r_far = jnp.concatenate([r[2][...], r[3][...], r[6][...], r[7][...]], axis=1)
    for zr in range(4):
        out = jnp.dot(la[zr][...], r_own, preferred_element_type=jnp.float32)
        for yr in range(4):
            acc[yr, z[0] ^ zr] = out[yr * 64:(yr + 1) * 64]
    for yr in range(4):
        out = jnp.dot(lb[yr][...], r_far, preferred_element_type=jnp.float32)
        for zr in range(4):
            at = z[0] ^ zr
            total = acc[yr, at] + out[zr * 64:(zr + 1) * 64]
            rows = pl.ds(pl.multiple_of(yr * 256 + at * 64, 64), 64)
            for part in range(2):
                keep[part, rows, :] = total[:, part * 128:part * 128 + 128]
                send[part, rows, :] = total[:, part * 128 + 256:part * 128 + 384]


def tile(z, la, lb, r):
    return pl.pallas_call(
        tile_kernel,
        out_shape=[jax.ShapeDtypeStruct((2, 1024, 128), jnp.float32)] * 2,
        in_specs=[SMEM] + [VMEM] * 16,
        out_specs=[VMEM] * 2,
        scratch_shapes=[pltpu.VMEM((4, 4, 64, 512), jnp.float32)],
        compiler_params=pltpu.CompilerParams(vmem_limit_bytes=40 * MIB),
        cost_estimate=pl.CostEstimate(flops=2 * 1024 * 2500 * 512, bytes_accessed=10 * MIB, transcendentals=0),
        name="tile",
    )(z, *la, *lb, *r)


def turn_kernel(keep, got, own, other):
    lane = lax.broadcasted_iota(jnp.int32, (16, 128), 1)
    odd = (lane // 32) % 2 == 1
    high = lane // 64 == 1
    for part, out in ((0, own), (1, other)):
        for group in range(16):
            v = []
            for c in range(4):
                rows = pl.ds(group * 4 + c, 16, stride=64)
                v.append(keep[part, rows, :] + got[part, rows, :])
            w = [
                jnp.where(odd, pltpu.roll(v[1], 32, 1), v[0]),
                jnp.where(odd, v[1], pltpu.roll(v[0], 96, 1)),
                jnp.where(odd, pltpu.roll(v[3], 32, 1), v[2]),
                jnp.where(odd, v[3], pltpu.roll(v[2], 96, 1)),
            ]
            t = [
                jnp.where(high, pltpu.roll(w[2], 64, 1), w[0]),
                jnp.where(high, pltpu.roll(w[3], 64, 1), w[1]),
                jnp.where(high, w[2], pltpu.roll(w[0], 64, 1)),
                jnp.where(high, w[3], pltpu.roll(w[1], 64, 1)),
            ]
            for b in range(4):
                out[b * 16:(b + 1) * 16, group * 128:(group + 1) * 128] = t[b].astype(jnp.bfloat16)


def turn(keep, got):
    return pl.pallas_call(
        turn_kernel,
        out_shape=[jax.ShapeDtypeStruct((64, 2048), jnp.bfloat16)] * 2,
        in_specs=[VMEM] * 2,
        out_specs=[VMEM] * 2,
        compiler_params=pltpu.CompilerParams(vmem_limit_bytes=16 * MIB),
        cost_estimate=pl.CostEstimate(flops=2 * MIB, bytes_accessed=3 * MIB, transcendentals=0),
        name="turn",
    )(keep, got)


def ladder_kernel(z, amp, *refs):
    parts, own, out, held = refs[:8], refs[8], refs[9:12], refs[12]
    for i in range(8):
        held[i * 64:(i + 1) * 64, :] = parts[i][...]
    for s in range(4):
        rows = pl.ds(pl.multiple_of((z[0] ^ s) * 256, 256), 256)
        part = dot_nt(amp[rows, :], held[...])
        if s == 0:
            own[...] = part
        else:
            out[s - 1][...] = part.astype(jnp.bfloat16)


def ladder(z, amp, parts):
    return pl.pallas_call(
        ladder_kernel,
        out_shape=[jax.ShapeDtypeStruct((256, 512), jnp.float32)] + [jax.ShapeDtypeStruct((256, 512), jnp.bfloat16)] * 3,
        in_specs=[SMEM] + [VMEM] * 9,
        out_specs=[VMEM] * 4,
        scratch_shapes=[pltpu.VMEM((512, 2048), jnp.bfloat16)],
        compiler_params=pltpu.CompilerParams(vmem_limit_bytes=32 * MIB),
        cost_estimate=pl.CostEstimate(flops=2 * 1024 * 2048 * 512, bytes_accessed=8 * MIB, transcendentals=0),
        name="ladder",
    )(z, amp, *parts)


def finish_kernel(own, r1, r2, r3, order, scale, out):
    total = own[...] + r1[...].astype(jnp.float32) + r2[...].astype(jnp.float32) + r3[...].astype(jnp.float32)
    turned = None
    for _ in range(3):
        term = total.astype(jnp.bfloat16)
        total = total - term.astype(jnp.float32)
        placed = jnp.dot(term, order[...], preferred_element_type=jnp.float32)
        turned = placed if turned is None else turned + placed
    out[...] = turned * scale[...]


def finish(own, got, order, scale):
    return pl.pallas_call(
        finish_kernel,
        out_shape=jax.ShapeDtypeStruct((256, 512), jnp.float32),
        in_specs=[VMEM] * 6,
        out_specs=VMEM,
        compiler_params=pltpu.CompilerParams(vmem_limit_bytes=16 * MIB),
        cost_estimate=pl.CostEstimate(flops=6 * 256 * 512 * 512, bytes_accessed=4 * MIB, transcendentals=0),
        name="finish",
    )(own, *got, order, scale)


def gather(x, axis):
    return [x] + [swap(x, **{axis: s}) for s in (1, 2, 3)]


def column_order(xh, core, y, xl):
    s = jnp.arange(512, dtype=jnp.int32)
    pc, px, b, yr, zr = s // 256, (s // 64) % 4, (s // 16) % 4, (s // 4) % 4, s % 4
    xl_of, xh_of = xl ^ (px % 2), xh ^ (px // 2)
    a = 16 * (y ^ yr) + 8 * xl_of + 2 * zr + xh_of
    target = (4 * (core ^ pc) + b) * 64 + a
    return (target[:, None] == jnp.arange(512, dtype=jnp.int32)[None, :]).astype(jnp.bfloat16)


def per_device(left, right, amplitudes, pair_list, offsets, occ_energy, virt_energy):
    rows, cols, z = (lax.axis_index(n) for n in AXES)
    xh, core, y, xl = rows // 2, rows % 2, cols // 2, cols % 2
    right = right.reshape(right.shape[0], 512)
    amp = amplitudes.reshape(1024, 2048)

    def group(j, mine):
        at = 2 * j + (core if mine else 1 - core)
        return lax.dynamic_slice(right, (0, at * 128), (right.shape[0], 128))

    r = []
    for j in range(CHUNKS):
        kept, sent = group(j, True), group(j, False)
        k1, s1 = swap(kept, xl=1), swap(sent, xl=1)
        k3, s3 = swap(kept, xl=1, xh=1), swap(sent, xl=1, xh=1)
        k2, s2 = swap(k1, xl=1, xh=1), swap(s3, xl=1)
        r.append((kept, k1, k2, k3, sent, s1, s2, s3))

    lt = left.T
    mine = lax.dynamic_slice(lt, (xh * 64, 0), (64, lt.shape[1]))
    theirs = lax.dynamic_slice(lt, ((1 - xh) * 64, 0), (64, lt.shape[1]))
    far = swap(theirs, xh=1)
    la = gather(jnp.concatenate(gather(mine, "y"), axis=0), "z")
    lb = gather(jnp.concatenate(gather(far, "z"), axis=0), "y")

    order = column_order(xh, core, y, xl)
    energy_a = lax.dynamic_slice(virt_energy, (offsets[0],), (A,))
    b_start = offsets[1] + cols * 16
    energy_b = lax.dynamic_slice(virt_energy, (b_start,), (16,))
    first = pair_list[:, 0:1]
    second = pair_list[:, 1:2]
    levels = jnp.arange(occ_energy.shape[0], dtype=jnp.int32)[None, :]
    occupied = jnp.sum(jnp.where(first == levels, occ_energy[None, :], 0.0), axis=1) + jnp.sum(
        jnp.where(second == levels, occ_energy[None, :], 0.0), axis=1
    )
    weight = jnp.where(pair_list[:, 0] == pair_list[:, 1], 0.5, 1.0).astype(jnp.float32)
    ab = (energy_b[:, None] + energy_a[None, :]).reshape(1, 1024)
    scale = weight[:, None] / (ab - occupied[:, None])

    zs = z.reshape(1).astype(jnp.int32)
    outs = []
    for j in range(CHUNKS):
        keep, send = tile(zs, la, lb, r[j])
        own, other = turn(keep, swap(send, core=1))
        mine4 = [own, swap(other, xl=1), swap(own, xh=1), swap(other, xl=1, xh=1)]
        parts = mine4 + [swap(v, core=1) for v in mine4]
        l0, l1, l2, l3 = ladder(zs, amp, parts)
        got = [swap(l1, z=1), swap(l2, z=2), swap(l3, z=3)]
        outs.append(finish(l0, got, order, scale[:, j * 512:(j + 1) * 512]))
    return jnp.concatenate(outs, axis=1)


def solution(mesh):
    placed = (
        P("rows", ("cols", "depth")),
        P("rows", "depth", "cols"),
        P("rows", "depth", None),
        P(("rows", "depth"), None),
        P(),
        P(),
        P(),
    )
    return jax.shard_map(
        per_device,
        mesh=mesh,
        in_specs=placed,
        out_specs=P(("rows", "depth"), "cols"),
        check_vma=False,
    )
```

```python
import functools

import jax
import jax.numpy as jnp
import numpy as np
from jax import lax
from jax.experimental import pallas as pl
from jax.experimental.pallas import tpu as pltpu
from jax.sharding import PartitionSpec as P

CHUNKS = 2
AXES = ("xh", "core", "y", "xl", "z")
SHAPE = (2, 2, 4, 2, 4)
VMEM = pl.BlockSpec(memory_space=pltpu.VMEM)
SMEM = pl.BlockSpec(memory_space=pltpu.SMEM)
HBM = pl.BlockSpec(memory_space=pltpu.HBM)
MIB = 1 << 20
BF16 = jnp.bfloat16
F32 = jnp.float32
XH, CORE, Y, XL, Z = range(5)


def swap_table(xh=0, core=0, y=0, xl=0, z=0):
    by = (xh, core, y, xl, z)
    table = []
    for i in range(128):
        to = tuple(int(v) ^ w for v, w in zip(np.unravel_index(i, SHAPE), by))
        table.append((i, int(np.ravel_multi_index(to, SHAPE))))
    return table


def swap(x, **by):
    return lax.ppermute(x, AXES, swap_table(**by))


def dot_nt(u, v):
    return lax.dot_general(u, v, (((1,), (1,)), ((), ())), preferred_element_type=jnp.float32)


def call(body, shapes, inputs, places, name, out_place=None, scratch=(), limit=4, flops=0, size=MIB, **more):
    many = isinstance(shapes, list)
    shapes = shapes if many else [shapes]
    got = pl.pallas_call(
        body,
        out_shape=[jax.ShapeDtypeStruct(*v) for v in shapes],
        in_specs=places,
        out_specs=[out_place or VMEM] * len(shapes),
        scratch_shapes=list(scratch),
        compiler_params=pltpu.CompilerParams(vmem_limit_bytes=limit * MIB),
        cost_estimate=pl.CostEstimate(flops=flops, bytes_accessed=size, transcendentals=0),
        name=name,
        **more,
    )(*inputs)
    return got if many else got[0]


def split_kernel(at, left, mine, theirs):
    t = left[...].T
    upper, lower = t[:64], t[64:]
    mine[...] = jnp.where(at[XH] == 0, upper, lower)
    theirs[...] = jnp.where(at[XH] == 0, lower, upper)


def split(at, left):
    return call(split_kernel, [((64, 1280), BF16)] * 2, (at, left), [SMEM, VMEM], "split")


def cut_kernel(cuts, source, *refs):
    for cut, out in zip(cuts, refs[len(refs) - len(cuts):]):
        out[...] = source[cut]


def cut(source, cuts, after=()):
    shapes = [(tuple(len(range(n)[c]) for c, n in zip(cut, source.shape)), BF16) for cut in cuts]
    return call(functools.partial(cut_kernel, cuts), shapes, (source, *after), [VMEM] + [HBM] * len(after), "cut")


def stack_kernel(n, *refs):
    for i in range(n):
        refs[-1][i * 64:(i + 1) * 64, :] = refs[i][...]


def stack(pieces, after=()):
    n = len(pieces)
    shape = ((64 * n, pieces[0].shape[1]), BF16)
    return call(functools.partial(stack_kernel, n), shape, (*pieces, *after), [VMEM] * n + [HBM] * len(after), "stack")


def tile_kernel(at, *refs):
    la, lb, r = refs[0:5], refs[5:10], refs[10:15]
    keep, send, acc = refs[-3:]
    first = at[CORE] == 0
    place = ((0, 0, 4), (1, 0, 4), (3, 0, 4), (2, 0, 2), (2, 2, 2))
    for part in range(2):
        right = r[part][...]
        for k, (zr, start, count) in enumerate(place):
            out = jnp.dot(la[k][:, :1250], right, preferred_element_type=jnp.float32)
            for i in range(count):
                acc[part, start + i, at[Z] ^ zr] = out[i * 64:(i + 1) * 64]
    for part in range(2):
        right = jnp.concatenate([r[3][...], r[4][...]], axis=1) if part == 0 else r[2][...]
        for k, (yr, start, count) in enumerate(place):
            out = jnp.dot(lb[k][:, :1250], right, preferred_element_type=jnp.float32)
            for i in range(count):
                zs = at[Z] ^ (start + i)
                total = acc[part, yr, zs] + out[i * 64:(i + 1) * 64]
                rows = pl.ds(pl.multiple_of(yr * 256 + zs * 64, 64), 64)
                keep[part, rows, :] = jnp.where(first, total[:, :128], total[:, 128:])
                send[part, rows, :] = jnp.where(first, total[:, 128:], total[:, :128])


def tile(at, la, lb, r, after=()):
    return call(
        tile_kernel,
        [((2, 1024, 128), F32)] * 2,
        (at, *la, *lb, *r, *after),
        [SMEM] + [VMEM] * 15 + [HBM] * len(after),
        "tile",
        scratch=[pltpu.VMEM((2, 4, 4, 64, 256), F32)],
        limit=6,
        flops=2 * 1024 * 2500 * 512,
        size=10 * MIB,
    )


def turn_kernel(keep, got, own, other):
    lane = lax.broadcasted_iota(jnp.int32, (16, 128), 1)
    odd = (lane // 32) % 2 == 1
    high = lane // 64 == 1
    for part, out in ((0, own), (1, other)):
        for group in range(16):
            v = []
            for c in range(4):
                rows = pl.ds(group * 4 + c, 16, stride=64)
                v.append(keep[part, rows, :] + got[part, rows, :])
            w = [
                jnp.where(odd, pltpu.roll(v[1], 32, 1), v[0]),
                jnp.where(odd, v[1], pltpu.roll(v[0], 96, 1)),
                jnp.where(odd, pltpu.roll(v[3], 32, 1), v[2]),
                jnp.where(odd, v[3], pltpu.roll(v[2], 96, 1)),
            ]
            t = [
                jnp.where(high, pltpu.roll(w[2], 64, 1), w[0]),
                jnp.where(high, pltpu.roll(w[3], 64, 1), w[1]),
                jnp.where(high, w[2], pltpu.roll(w[0], 64, 1)),
                jnp.where(high, w[3], pltpu.roll(w[1], 64, 1)),
            ]
            for b in range(4):
                out[b * 16:(b + 1) * 16, group * 128:(group + 1) * 128] = t[b].astype(jnp.bfloat16)


def turn(keep, got):
    return call(turn_kernel, [((64, 2048), BF16)] * 2, (keep, got), [VMEM] * 2, "turn", size=3 * MIB)


def ladder_kernel(at, amp, mine, peer, own, *out):
    for s in range(4):
        rows = pl.ds(pl.multiple_of((at[Z] ^ s) * 256, 256), 256)
        for k, part in enumerate((mine, peer)):
            lanes = slice(k * 256, (k + 1) * 256)
            total = dot_nt(amp[rows, :], part[...])
            if s == 0:
                own[:, lanes] = total
            else:
                out[s - 1][:, lanes] = total.astype(BF16)


def ladder(at, amp, mine, peer):
    shapes = [((256, 512), F32)] + [((256, 512), BF16)] * 3
    inputs = (at, amp, mine, peer)
    return call(ladder_kernel, shapes, inputs, [SMEM] + [VMEM] * 3, "ladder", flops=2 * 1024 * 2048 * 512, size=8 * MIB)


def finish_kernel(j, own, r1, r2, r3, order, scale, *refs):
    out, held, sem = refs[-3:]
    total = own[...] + r1[...].astype(F32) + r2[...].astype(F32) + r3[...].astype(F32)
    turned = None
    for _ in range(3):
        term = total.astype(BF16)
        total = total - term.astype(F32)
        placed = jnp.dot(term, order[...], preferred_element_type=F32)
        turned = placed if turned is None else turned + placed
    lanes = pl.ds(j * 512, 512)
    held[...] = turned * scale[:, lanes]
    copy = pltpu.make_async_copy(held, out.at[:, lanes], sem)
    copy.start()
    copy.wait()


def finish(j, own, got, order, scale, out):
    before = [] if out is None else [out]
    return call(
        functools.partial(finish_kernel, j),
        ((256, 1024), F32),
        (own, *got, order, scale, *before),
        [VMEM] * 6 + [HBM] * len(before),
        "finish",
        out_place=HBM,
        scratch=[pltpu.VMEM((256, 512), F32), pltpu.SemaphoreType.DMA],
        flops=6 * 256 * 512 * 512,
        size=4 * MIB,
        input_output_aliases={6: 0} if before else {},
    )


def prepare_kernel(at, offsets, virt, pairs, occ, order, scale):
    s = lax.broadcasted_iota(jnp.int32, (512, 1), 0)
    pc, px, b, yr, zr = s // 256, (s // 64) % 4, (s // 16) % 4, (s // 4) % 4, s % 4
    xl, xh = at[XL] ^ (px % 2), at[XH] ^ (px // 2)
    target = (4 * (at[CORE] ^ pc) + b) * 64 + 16 * (at[Y] ^ yr) + 8 * xl + 2 * zr + xh
    columns = lax.broadcasted_iota(jnp.int32, (512, 512), 1)
    order[...] = jnp.where(columns == target, 1.0, 0.0).astype(BF16)

    lane = lax.broadcasted_iota(jnp.int32, (8, 128), 1)
    ea = jnp.zeros((8, 128), F32)
    for a in range(64):
        ea = jnp.where(lane % 64 == a, virt[offsets[0] + a], ea)
    b_start = offsets[1] + (at[Y] * 2 + at[XL]) * 16
    first, second = pairs[:, 0:1], pairs[:, 1:2]
    levels = lax.broadcasted_iota(jnp.int32, (256, 120), 1)
    occupied = jnp.sum(jnp.where(levels == first, occ[...], 0.0), axis=1, keepdims=True)
    occupied += jnp.sum(jnp.where(levels == second, occ[...], 0.0), axis=1, keepdims=True)
    weight = jnp.where(first == second, 0.5, 1.0)
    for b in range(0, 16, 2):
        eb = jnp.where(lane < 64, virt[b_start + b], virt[b_start + b + 1])
        scale[:, b * 64:(b + 2) * 64] = weight / ((eb + ea)[:1] - occupied)


def prepare(at, offsets, virt, pairs, occ):
    return call(
        prepare_kernel,
        [((512, 512), BF16), ((256, 1024), F32)],
        (at, offsets, virt, pairs, occ.reshape(1, -1)),
        [SMEM] * 3 + [VMEM] * 2,
        "prepare",
    )


def spread(x, axis):
    one, three = swap(x, **{axis: 1}), swap(x, **{axis: 3})
    (upper,), (lower,) = cut(one, [np.s_[:128, :]]), cut(three, [np.s_[128:, :]])
    return [x, one, three, swap(upper, **{axis: 3}), swap(lower, **{axis: 1})]


def around(x):
    one, three = swap(x, xl=1), swap(x, xl=1, xh=1)
    (near,), (far,) = cut(one, [np.s_[:, :128]]), cut(three, [np.s_[:, 128:]])
    return [x, one, three, swap(near, xl=1, xh=1), swap(far, xl=1)]


def per_device(left, right, amplitudes, pair_list, offsets, occ_energy, virt_energy):
    at = jnp.stack([lax.axis_index(n) for n in AXES]).astype(jnp.int32)
    right = right.reshape(right.shape[0], 512)
    amp = amplitudes.reshape(1024, 2048)

    mine, theirs = split(at, jnp.pad(left, ((0, 30), (0, 0))))
    far = swap(theirs, xh=1)
    mine = stack([mine], (far,))
    far4 = [far] + [swap(far, z=s) for s in (1, 2, 3)]
    mine4 = [mine] + [swap(mine, y=s) for s in (1, 2, 3)]
    la = spread(stack(mine4, tuple(far4[1:])), "z")
    lb = spread(stack(far4, tuple(mine4[1:])), "y")

    r = [around(v) for v in cut(right, [np.s_[:, :256], np.s_[:, 256:]], (far,))]
    order, scale = prepare(at, offsets, virt_energy, pair_list, occ_energy)

    turned, after = [], ()
    for j in range(CHUNKS):
        keep, send = tile(at, la, lb, r[j], after)
        turned.append(turn(keep, swap(send, core=1)))
    out, after = None, (turned[1][0],)
    for j in range(CHUNKS):
        own, other = turned[j]
        held = stack([own, swap(other, xl=1), swap(own, xh=1), swap(other, xl=1, xh=1)], after)
        l0, l1, l2, l3 = ladder(at, amp, held, swap(held, core=1))
        got = [swap(l1, z=1), swap(l2, z=2), swap(l3, z=3)]
        after = (got[0], got[2])
        out = finish(j, l0, got, order, scale, out)
    return out


def solution(mesh):
    mesh = jax.sharding.Mesh(mesh.devices.reshape(SHAPE), AXES)
    rows, cols = ("xh", "core"), ("y", "xl")
    placed = (
        P(rows, (*cols, "z")),
        P(rows, "z", cols),
        P(rows, "z", None),
        P((*rows, "z"), None),
        P(),
        P(),
        P(),
    )
    return jax.shard_map(
        per_device,
        mesh=mesh,
        in_specs=placed,
        out_specs=P((*rows, "z"), cols),
        check_vma=False,
    )
```

```python
import functools

import jax
import jax.numpy as jnp
import numpy as np
from jax import lax
from jax.experimental import pallas as pl
from jax.experimental.pallas import tpu as pltpu
from jax.sharding import PartitionSpec as P

CHUNKS = 2
AXES = ("xh", "core", "y", "xl", "z")
SHAPE = (2, 2, 4, 2, 4)
VMEM = pl.BlockSpec(memory_space=pltpu.VMEM)
SMEM = pl.BlockSpec(memory_space=pltpu.SMEM)
HBM = pl.BlockSpec(memory_space=pltpu.HBM)
MIB = 1 << 20
BF16 = jnp.bfloat16
F32 = jnp.float32
XH, CORE, Y, XL, Z = range(5)


def swap_table(xh=0, core=0, y=0, xl=0, z=0):
    by = (xh, core, y, xl, z)
    table = []
    for i in range(128):
        to = tuple(int(v) ^ w for v, w in zip(np.unravel_index(i, SHAPE), by))
        table.append((i, int(np.ravel_multi_index(to, SHAPE))))
    return table


def swap(x, **by):
    return lax.ppermute(x, AXES, swap_table(**by))


def dot_nt(u, v):
    return lax.dot_general(u, v, (((1,), (1,)), ((), ())), preferred_element_type=jnp.float32)


def call(body, shapes, inputs, places, name, out_place=None, scratch=(), limit=4, flops=0, size=MIB, **more):
    many = isinstance(shapes, list)
    shapes = shapes if many else [shapes]
    got = pl.pallas_call(
        body,
        out_shape=[jax.ShapeDtypeStruct(*v) for v in shapes],
        in_specs=places,
        out_specs=[out_place or VMEM] * len(shapes),
        scratch_shapes=list(scratch),
        compiler_params=pltpu.CompilerParams(vmem_limit_bytes=limit * MIB),
        cost_estimate=pl.CostEstimate(flops=flops, bytes_accessed=size, transcendentals=0),
        name=name,
        **more,
    )(*inputs)
    return got if many else got[0]


def split_kernel(at, left, mine, theirs):
    t = left[...].T
    upper, lower = t[:64], t[64:]
    mine[...] = jnp.where(at[XH] == 0, upper, lower)
    theirs[...] = jnp.where(at[XH] == 0, lower, upper)


def split(at, left):
    return call(split_kernel, [((64, 1280), BF16)] * 2, (at, left), [SMEM, VMEM], "split")


def cut_kernel(cuts, source, *refs):
    for cut, out in zip(cuts, refs[len(refs) - len(cuts):]):
        out[...] = source[cut]


def cut(source, cuts, after=()):
    shapes = [(tuple(len(range(n)[c]) for c, n in zip(cut, source.shape)), BF16) for cut in cuts]
    return call(functools.partial(cut_kernel, cuts), shapes, (source, *after), [VMEM] + [HBM] * len(after), "cut")


def stack_kernel(n, *refs):
    for i in range(n):
        refs[-1][i * 64:(i + 1) * 64, :] = refs[i][...]


def stack(pieces, after=()):
    n = len(pieces)
    shape = ((64 * n, pieces[0].shape[1]), BF16)
    return call(functools.partial(stack_kernel, n), shape, (*pieces, *after), [VMEM] * n + [HBM] * len(after), "stack")


def tile_kernel(j, at, *refs):
    la, lb, r = refs[0:5], refs[5:10], refs[10:15]
    keep, send, acc = refs[-3:]
    first = at[CORE] == 0
    lanes = slice(j * 128, (j + 1) * 128)
    place = ((0, 0, 4), (1, 0, 4), (3, 0, 4), (2, 0, 2), (2, 2, 2))
    for part in range(2):
        right = r[part][...]
        for k, (zr, start, count) in enumerate(place):
            out = jnp.dot(la[k][:, :1250], right, preferred_element_type=jnp.float32)
            for i in range(count):
                acc[part, start + i, at[Z] ^ zr] = out[i * 64:(i + 1) * 64]
    for part in range(2):
        right = jnp.concatenate([r[3][:, lanes], r[4][:, lanes]], axis=1) if part == 0 else r[2][...]
        for k, (yr, start, count) in enumerate(place):
            out = jnp.dot(lb[k][:, :1250], right, preferred_element_type=jnp.float32)
            for i in range(count):
                zs = at[Z] ^ (start + i)
                total = acc[part, yr, zs] + out[i * 64:(i + 1) * 64]
                rows = pl.ds(pl.multiple_of(yr * 256 + zs * 64, 64), 64)
                keep[part, rows, :] = jnp.where(first, total[:, :128], total[:, 128:])
                send[part, rows, :] = jnp.where(first, total[:, 128:], total[:, :128])


def tile(j, at, la, lb, r, after=()):
    return call(
        functools.partial(tile_kernel, j),
        [((2, 1024, 128), F32)] * 2,
        (at, *la, *lb, *r, *after),
        [SMEM] + [VMEM] * 15 + [HBM] * len(after),
        "tile",
        scratch=[pltpu.VMEM((2, 4, 4, 64, 256), F32)],
        limit=6,
        flops=2 * 1024 * 2500 * 512,
        size=10 * MIB,
    )


def turn_kernel(keep, got, own, other, total):
    lane = lax.broadcasted_iota(jnp.int32, (16, 128), 1)
    odd = (lane // 32) % 2 == 1
    high = lane // 64 == 1
    total[...] = keep[...] + got[...]
    for part, out in ((0, own), (1, other)):
        for group in range(16):
            v = []
            for c in range(4):
                rows = pl.ds(group * 4 + c, 16, stride=64)
                v.append(total[part, rows, :])
            w = [
                jnp.where(odd, pltpu.roll(v[1], 32, 1), v[0]),
                jnp.where(odd, v[1], pltpu.roll(v[0], 96, 1)),
                jnp.where(odd, pltpu.roll(v[3], 32, 1), v[2]),
                jnp.where(odd, v[3], pltpu.roll(v[2], 96, 1)),
            ]
            t = [
                jnp.where(high, pltpu.roll(w[2], 64, 1), w[0]),
                jnp.where(high, pltpu.roll(w[3], 64, 1), w[1]),
                jnp.where(high, w[2], pltpu.roll(w[0], 64, 1)),
                jnp.where(high, w[3], pltpu.roll(w[1], 64, 1)),
            ]
            for b in range(4):
                out[b * 16:(b + 1) * 16, group * 128:(group + 1) * 128] = t[b].astype(jnp.bfloat16)


def turn(keep, got):
    return call(turn_kernel, [((64, 2048), BF16)] * 2, (keep, got), [VMEM] * 2, "turn", scratch=[pltpu.VMEM((2, 1024, 128), F32)], size=3 * MIB)


def ladder_kernel(at, amp, part, *refs):
    halves, outs = refs[:-4], refs[-4:]
    for s, out in enumerate(outs):
        rows = pl.ds(pl.multiple_of((at[Z] ^ s) * 256, 256), 256)
        total = dot_nt(amp[rows, :], part[...]).astype(out.dtype)
        if halves:
            out[:, :256] = halves[s][...]
            out[:, 256:] = total
        else:
            out[...] = total


def ladder(at, amp, part, halves=()):
    shape = (256, 512 if halves else 256)
    return call(
        ladder_kernel,
        [(shape, F32)] + [(shape, BF16)] * 3,
        (at, amp, part, *halves),
        [SMEM] + [VMEM] * (2 + len(halves)),
        "ladder",
        flops=2 * 1024 * 2048 * 256,
        size=6 * MIB,
    )


def finish_kernel(j, own, r1, r2, r3, order, scale, *refs):
    out, held, sem = refs[-3:]
    total = own[...] + r1[...].astype(F32) + r2[...].astype(F32) + r3[...].astype(F32)
    turned = None
    for _ in range(3):
        term = total.astype(BF16)
        total = total - term.astype(F32)
        placed = jnp.dot(term, order[...], preferred_element_type=F32)
        turned = placed if turned is None else turned + placed
    lanes = pl.ds(j * 512, 512)
    held[...] = turned * scale[:, lanes]
    copy = pltpu.make_async_copy(held, out.at[:, lanes], sem)
    copy.start()
    copy.wait()


def finish(j, own, got, order, scale, out):
    before = [] if out is None else [out]
    return call(
        functools.partial(finish_kernel, j),
        ((256, 1024), F32),
        (own, *got, order, scale, *before),
        [VMEM] * 6 + [HBM] * len(before),
        "finish",
        out_place=HBM,
        scratch=[pltpu.VMEM((256, 512), F32), pltpu.SemaphoreType.DMA],
        flops=6 * 256 * 512 * 512,
        size=4 * MIB,
        input_output_aliases={6: 0} if before else {},
    )


def prepare_kernel(at, offsets, virt, pairs, occ, order, scale):
    s = lax.broadcasted_iota(jnp.int32, (512, 1), 0)
    pc, px, b, yr, zr = s // 256, (s // 64) % 4, (s // 16) % 4, (s // 4) % 4, s % 4
    xl, xh = at[XL] ^ (px % 2), at[XH] ^ (px // 2)
    target = (4 * (at[CORE] ^ pc) + b) * 64 + 16 * (at[Y] ^ yr) + 8 * xl + 2 * zr + xh
    columns = lax.broadcasted_iota(jnp.int32, (512, 512), 1)
    order[...] = jnp.where(columns == target, 1.0, 0.0).astype(BF16)

    lane = lax.broadcasted_iota(jnp.int32, (8, 128), 1)
    ea = jnp.zeros((8, 128), F32)
    for a in range(64):
        ea = jnp.where(lane % 64 == a, virt[offsets[0] + a], ea)
    b_start = offsets[1] + (at[Y] * 2 + at[XL]) * 16
    first, second = pairs[:, 0:1], pairs[:, 1:2]
    levels = lax.broadcasted_iota(jnp.int32, (256, 120), 1)
    occupied = jnp.sum(jnp.where(levels == first, occ[...], 0.0), axis=1, keepdims=True)
    occupied += jnp.sum(jnp.where(levels == second, occ[...], 0.0), axis=1, keepdims=True)
    weight = jnp.where(first == second, 0.5, 1.0)
    for b in range(0, 16, 2):
        eb = jnp.where(lane < 64, virt[b_start + b], virt[b_start + b + 1])
        scale[:, b * 64:(b + 2) * 64] = weight / ((eb + ea)[:1] - occupied)


def prepare(at, offsets, virt, pairs, occ):
    return call(
        prepare_kernel,
        [((512, 512), BF16), ((256, 1024), F32)],
        (at, offsets, virt, pairs, occ.reshape(1, -1)),
        [SMEM] * 3 + [VMEM] * 2,
        "prepare",
    )


def join_kernel(lanes, *refs):
    refs[-1][...] = jnp.concatenate([v[:, lanes] for v in refs[:-1]], axis=1)


def join(parts, lanes):
    shape = ((parts[0].shape[0], 128 * len(parts)), BF16)
    return call(functools.partial(join_kernel, lanes), shape, parts, [VMEM] * len(parts), "join")


def spread(x, axis, after):
    one, three = swap(x, **{axis: 1}), swap(x, **{axis: 3})
    (upper,), (lower,) = cut(one, [np.s_[:128, :]], after), cut(three, [np.s_[128:, :]], after)
    return [x, one, three, swap(upper, **{axis: 3}), swap(lower, **{axis: 1})]


def per_device(left, right, amplitudes, pair_list, offsets, occ_energy, virt_energy):
    at = jnp.stack([lax.axis_index(n) for n in AXES]).astype(jnp.int32)
    right = right.reshape(right.shape[0], 512)
    amp = amplitudes.reshape(1024, 2048)

    mine, theirs = split(at, jnp.pad(left, ((0, 30), (0, 0))))
    far = swap(theirs, xh=1)
    r0 = cut(right, [np.s_[:, :256]], (theirs,))
    mine = stack([mine], r0)
    far4 = [far] + [swap(far, z=s) for s in (1, 2, 3)]
    mine4 = [mine] + [swap(mine, y=s) for s in (1, 2, 3)]
    r0 += cut(right, [np.s_[:, 256:]], (mine4[3], far4[1]))
    r1, r3 = [swap(v, xl=1) for v in r0], [swap(v, xl=1, xh=1) for v in r0]

    la = stack(mine4, (*far4[1:], r1[0], r3[0]))
    lb = stack(far4, (*mine4[1:], r1[0], r3[0]))
    la, lb = spread(la, "z", (r1[1], r3[1])), spread(lb, "y", (r1[1], r3[1]))
    r2 = swap(join(r1, np.s_[:128]), xl=1, xh=1), swap(join(r3, np.s_[128:]), xl=1)
    order, scale = prepare(at, offsets, virt_energy, pair_list, occ_energy)

    parts = []
    for j in range(CHUNKS):
        keep, send = tile(j, at, la, lb, (r0[j], r1[j], r3[j], *r2))
        own, other = turn(keep, swap(send, core=1))
        parts.append([own, swap(other, xl=1), swap(own, xh=1), swap(other, xl=1, xh=1)])
    out, after = None, (parts[1][1], parts[1][3])
    for j in range(CHUNKS):
        held = stack(parts[j], after)
        peer = swap(held, core=1)
        l0, l1, l2, l3 = ladder(at, amp, peer, ladder(at, amp, held))
        got = [swap(l1, z=1), swap(l3, z=3), swap(l2, z=2)]
        after = (got[0], got[1])
        out = finish(j, l0, got, order, scale, out)
    return out


def solution(mesh):
    mesh = jax.sharding.Mesh(mesh.devices.reshape(SHAPE), AXES)
    rows, cols = ("xh", "core"), ("y", "xl")
    placed = (
        P(rows, (*cols, "z")),
        P(rows, "z", cols),
        P(rows, "z", None),
        P((*rows, "z"), None),
        P(),
        P(),
        P(),
    )
    return jax.shard_map(
        per_device,
        mesh=mesh,
        in_specs=placed,
        out_specs=P((*rows, "z"), cols),
        check_vma=False,
    )
```

```python
import functools

import jax
import jax.numpy as jnp
import numpy as np
from jax import lax
from jax.experimental import pallas as pl
from jax.experimental.pallas import tpu as pltpu
from jax.sharding import PartitionSpec as P

CHUNKS = 2
AXES = ("xh", "core", "y", "xl", "z")
SHAPE = (2, 2, 4, 2, 4)
VMEM = pl.BlockSpec(memory_space=pltpu.VMEM)
SMEM = pl.BlockSpec(memory_space=pltpu.SMEM)
HBM = pl.BlockSpec(memory_space=pltpu.HBM)
MIB = 1 << 20
BF16 = jnp.bfloat16
F32 = jnp.float32
XH, CORE, Y, XL, Z = range(5)


def swap_table(xh=0, core=0, y=0, xl=0, z=0):
    by = (xh, core, y, xl, z)
    table = []
    for i in range(128):
        to = tuple(int(v) ^ w for v, w in zip(np.unravel_index(i, SHAPE), by))
        table.append((i, int(np.ravel_multi_index(to, SHAPE))))
    return table


def swap(x, **by):
    return lax.ppermute(x, AXES, swap_table(**by))


def dot_nt(u, v):
    return lax.dot_general(u, v, (((1,), (1,)), ((), ())), preferred_element_type=jnp.float32)


def call(body, shapes, inputs, places, name, out_place=None, scratch=(), limit=4, flops=0, size=MIB, **more):
    many = isinstance(shapes, list)
    shapes = shapes if many else [shapes]
    got = pl.pallas_call(
        body,
        out_shape=[jax.ShapeDtypeStruct(*v) for v in shapes],
        in_specs=places,
        out_specs=[out_place or VMEM] * len(shapes),
        scratch_shapes=list(scratch),
        compiler_params=pltpu.CompilerParams(vmem_limit_bytes=limit * MIB),
        cost_estimate=pl.CostEstimate(flops=flops, bytes_accessed=size, transcendentals=0),
        name=name,
        **more,
    )(*inputs)
    return got if many else got[0]


def split_kernel(at, left, mine, theirs):
    t = left[...].T
    upper, lower = t[:64], t[64:]
    mine[...] = jnp.where(at[XH] == 0, upper, lower)
    theirs[...] = jnp.where(at[XH] == 0, lower, upper)


def split(at, left):
    return call(split_kernel, [((64, 1280), BF16)] * 2, (at, left), [SMEM, VMEM], "split")


def cut_kernel(cuts, source, *refs):
    for cut, out in zip(cuts, refs[len(refs) - len(cuts):]):
        out[...] = source[cut]


def cut(source, cuts, after=()):
    shapes = [(tuple(len(range(n)[c]) for c, n in zip(cut, source.shape)), BF16) for cut in cuts]
    return call(functools.partial(cut_kernel, cuts), shapes, (source, *after), [VMEM] + [HBM] * len(after), "cut")


def stack_kernel(n, *refs):
    for i in range(n):
        refs[-1][i * 64:(i + 1) * 64, :] = refs[i][...]


def stack(pieces, after=()):
    n = len(pieces)
    shape = ((64 * n, pieces[0].shape[1]), BF16)
    return call(functools.partial(stack_kernel, n), shape, (*pieces, *after), [VMEM] * n + [HBM] * len(after), "stack")


def tile_kernel(j, at, *refs):
    la, lb, r = refs[0:5], refs[5:10], refs[10:15]
    keep, send, acc = refs[-3:]
    first = at[CORE] == 0
    lanes = slice(j * 128, (j + 1) * 128)
    place = ((0, 0, 4), (1, 0, 4), (3, 0, 4), (2, 0, 2), (2, 2, 2))
    for part in range(2):
        right = r[part][...]
        for k, (zr, start, count) in enumerate(place):
            out = jnp.dot(la[k][:, :1250], right, preferred_element_type=jnp.float32)
            for i in range(count):
                acc[part, start + i, at[Z] ^ zr] = out[i * 64:(i + 1) * 64]
    for part in range(2):
        right = jnp.concatenate([r[3][:, lanes], r[4][:, lanes]], axis=1) if part == 0 else r[2][...]
        for k, (yr, start, count) in enumerate(place):
            out = jnp.dot(lb[k][:, :1250], right, preferred_element_type=jnp.float32)
            for i in range(count):
                zs = at[Z] ^ (start + i)
                total = acc[part, yr, zs] + out[i * 64:(i + 1) * 64]
                rows = pl.ds(pl.multiple_of(yr * 256 + zs * 64, 64), 64)
                keep[part, rows, :] = jnp.where(first, total[:, :128], total[:, 128:])
                send[part, rows, :] = jnp.where(first, total[:, 128:], total[:, :128])


def tile(j, at, la, lb, r, after=()):
    return call(
        functools.partial(tile_kernel, j),
        [((2, 1024, 128), F32)] * 2,
        (at, *la, *lb, *r, *after),
        [SMEM] + [VMEM] * 15 + [HBM] * len(after),
        "tile",
        scratch=[pltpu.VMEM((2, 4, 4, 64, 256), F32)],
        limit=6,
        flops=2 * 1024 * 2500 * 512,
        size=10 * MIB,
    )


def turn_kernel(keep, got, own, other, total):
    lane = lax.broadcasted_iota(jnp.int32, (16, 128), 1)
    odd = (lane // 32) % 2 == 1
    high = lane // 64 == 1
    total[...] = keep[...] + got[...]
    for part, out in ((0, own), (1, other)):
        for group in range(16):
            v = []
            for c in range(4):
                rows = pl.ds(group * 4 + c, 16, stride=64)
                v.append(total[part, rows, :])
            w = [
                jnp.where(odd, pltpu.roll(v[1], 32, 1), v[0]),
                jnp.where(odd, v[1], pltpu.roll(v[0], 96, 1)),
                jnp.where(odd, pltpu.roll(v[3], 32, 1), v[2]),
                jnp.where(odd, v[3], pltpu.roll(v[2], 96, 1)),
            ]
            t = [
                jnp.where(high, pltpu.roll(w[2], 64, 1), w[0]),
                jnp.where(high, pltpu.roll(w[3], 64, 1), w[1]),
                jnp.where(high, w[2], pltpu.roll(w[0], 64, 1)),
                jnp.where(high, w[3], pltpu.roll(w[1], 64, 1)),
            ]
            for b in range(4):
                out[b * 16:(b + 1) * 16, group * 128:(group + 1) * 128] = t[b].astype(jnp.bfloat16)


def turn(keep, got):
    return call(turn_kernel, [((64, 2048), BF16)] * 2, (keep, got), [VMEM] * 2, "turn", scratch=[pltpu.VMEM((2, 1024, 128), F32)], size=3 * MIB)


def ladder_kernel(at, amp, part, *refs):
    halves, outs = refs[:-3], refs[-3:]
    for s, out in enumerate(outs):
        rows = pl.ds(pl.multiple_of((at[Z] ^ (s + 1)) * 256, 256), 256)
        total = dot_nt(amp[rows, :], part[...]).astype(BF16)
        if halves:
            out[:, :256] = halves[s][...]
            out[:, 256:] = total
        else:
            out[...] = total


def ladder(at, amp, part, halves=()):
    shape = (256, 512 if halves else 256)
    return call(
        ladder_kernel,
        [(shape, BF16)] * 3,
        (at, amp, part, *halves),
        [SMEM] + [VMEM] * (2 + len(halves)),
        "ladder",
        flops=2 * 768 * 2048 * 256,
        size=4 * MIB,
    )


def own_kernel(at, amp, mine, peer, *refs):
    rows = pl.ds(pl.multiple_of(at[Z] * 256, 256), 256)
    for k, part in enumerate((mine, peer)):
        refs[-1][:, k * 256:(k + 1) * 256] = dot_nt(amp[rows, :], part[...])


def own_ladder(at, amp, mine, peer, after):
    inputs = (at, amp, mine, peer, *after)
    places = [SMEM] + [VMEM] * 3 + [HBM] * len(after)
    return call(own_kernel, ((256, 512), F32), inputs, places, "own", flops=2 * 256 * 2048 * 512, size=4 * MIB)


def finish_kernel(j, own, r1, r2, r3, order, scale, *refs):
    out, held, sem = refs[-3:]
    total = own[...] + r1[...].astype(F32) + r2[...].astype(F32) + r3[...].astype(F32)
    turned = None
    for _ in range(3):
        term = total.astype(BF16)
        total = total - term.astype(F32)
        placed = jnp.dot(term, order[...], preferred_element_type=F32)
        turned = placed if turned is None else turned + placed
    lanes = pl.ds(j * 512, 512)
    held[...] = turned * scale[:, lanes]
    copy = pltpu.make_async_copy(held, out.at[:, lanes], sem)
    copy.start()
    copy.wait()


def finish(j, own, got, order, scale, out):
    before = [] if out is None else [out]
    return call(
        functools.partial(finish_kernel, j),
        ((256, 1024), F32),
        (own, *got, order, scale, *before),
        [VMEM] * 6 + [HBM] * len(before),
        "finish",
        out_place=HBM,
        scratch=[pltpu.VMEM((256, 512), F32), pltpu.SemaphoreType.DMA],
        flops=6 * 256 * 512 * 512,
        size=4 * MIB,
        input_output_aliases={6: 0} if before else {},
    )


def prepare_kernel(at, offsets, virt, pairs, occ, order, scale):
    s = lax.broadcasted_iota(jnp.int32, (512, 1), 0)
    pc, px, b, yr, zr = s // 256, (s // 64) % 4, (s // 16) % 4, (s // 4) % 4, s % 4
    xl, xh = at[XL] ^ (px % 2), at[XH] ^ (px // 2)
    target = (4 * (at[CORE] ^ pc) + b) * 64 + 16 * (at[Y] ^ yr) + 8 * xl + 2 * zr + xh
    columns = lax.broadcasted_iota(jnp.int32, (512, 512), 1)
    order[...] = jnp.where(columns == target, 1.0, 0.0).astype(BF16)

    lane = lax.broadcasted_iota(jnp.int32, (8, 128), 1)
    ea = jnp.zeros((8, 128), F32)
    for a in range(64):
        ea = jnp.where(lane % 64 == a, virt[offsets[0] + a], ea)
    b_start = offsets[1] + (at[Y] * 2 + at[XL]) * 16
    first, second = (jnp.broadcast_to(pairs[i:i + 1, :], (8, 256)).T[:, 0:1] for i in (0, 1))
    levels = lax.broadcasted_iota(jnp.int32, (256, 120), 1)
    occupied = jnp.sum(jnp.where(levels == first, occ[...], 0.0), axis=1, keepdims=True)
    occupied += jnp.sum(jnp.where(levels == second, occ[...], 0.0), axis=1, keepdims=True)
    weight = jnp.where(first == second, 0.5, 1.0)
    for b in range(0, 16, 2):
        eb = jnp.where(lane < 64, virt[b_start + b], virt[b_start + b + 1])
        scale[:, b * 64:(b + 2) * 64] = weight / ((eb + ea)[:1] - occupied)


def prepare(at, offsets, virt, pairs, occ):
    return call(
        prepare_kernel,
        [((512, 512), BF16), ((256, 1024), F32)],
        (at, offsets, virt, pairs.T, occ.reshape(1, -1)),
        [SMEM] * 3 + [VMEM] * 2,
        "prepare",
    )


def join_kernel(lanes, *refs):
    refs[-1][...] = jnp.concatenate([v[:, lanes] for v in refs[:-1]], axis=1)


def join(parts, lanes):
    shape = ((parts[0].shape[0], 128 * len(parts)), BF16)
    return call(functools.partial(join_kernel, lanes), shape, parts, [VMEM] * len(parts), "join")


def spread(x, axis, after):
    one, three = swap(x, **{axis: 1}), swap(x, **{axis: 3})
    (upper,), (lower,) = cut(one, [np.s_[:128, :]], after), cut(three, [np.s_[128:, :]], after)
    return [x, one, three, swap(upper, **{axis: 3}), swap(lower, **{axis: 1})]


def per_device(left, right, amplitudes, pair_list, offsets, occ_energy, virt_energy):
    at = jnp.stack([lax.axis_index(n) for n in AXES]).astype(jnp.int32)
    right = right.reshape(right.shape[0], 512)
    amp = amplitudes.reshape(1024, 2048)

    mine, theirs = split(at, jnp.pad(left, ((0, 30), (0, 0))))
    far = swap(theirs, xh=1)
    r0 = cut(right, [np.s_[:, :256]], (theirs,))
    mine = stack([mine], r0)
    far4 = [far] + [swap(far, z=s) for s in (1, 2, 3)]
    mine4 = [mine] + [swap(mine, y=s) for s in (1, 2, 3)]
    r0 += cut(right, [np.s_[:, 256:]], (mine4[3], far4[1]))
    r1, r3 = [swap(v, xl=1) for v in r0], [swap(v, xl=1, xh=1) for v in r0]

    la = stack(mine4, (*far4[1:], r1[0], r3[0]))
    lb = stack(far4, (*mine4[1:], r1[0], r3[0]))
    la, lb = spread(la, "z", (r1[1], r3[1])), spread(lb, "y", (r1[1], r3[1]))
    r2 = swap(join(r1, np.s_[:128]), xl=1, xh=1), swap(join(r3, np.s_[128:]), xl=1)
    order, scale = prepare(at, offsets, virt_energy, pair_list, occ_energy)

    parts = []
    for j in range(CHUNKS):
        keep, send = tile(j, at, la, lb, (r0[j], r1[j], r3[j], *r2))
        own, other = turn(keep, swap(send, core=1))
        parts.append([own, swap(other, xl=1), swap(own, xh=1), swap(other, xl=1, xh=1)])
    out, after = None, (parts[1][1], parts[1][3])
    for j in range(CHUNKS):
        held = stack(parts[j], after)
        peer = swap(held, core=1)
        l1, l2, l3 = ladder(at, amp, peer, ladder(at, amp, held))
        l0 = own_ladder(at, amp, held, peer, (l1,))
        got = [swap(l1, z=1), swap(l3, z=3), swap(l2, z=2)]
        after = (got[0], got[1])
        out = finish(j, l0, got, order, scale, out)
    return out


def solution(mesh):
    mesh = jax.sharding.Mesh(mesh.devices.reshape(SHAPE), AXES)
    rows, cols = ("xh", "core"), ("y", "xl")
    placed = (
        P(rows, (*cols, "z")),
        P(rows, "z", cols),
        P(rows, "z", None),
        P((*rows, "z"), None),
        P(),
        P(),
        P(),
    )
    return jax.shard_map(
        per_device,
        mesh=mesh,
        in_specs=placed,
        out_specs=P((*rows, "z"), cols),
        check_vma=False,
    )
```

```python
import functools

import jax
import jax.numpy as jnp
import numpy as np
from jax import lax
from jax.experimental import pallas as pl
from jax.experimental.pallas import tpu as pltpu
from jax.sharding import PartitionSpec as P

CHUNKS = 2
AXES = ("xh", "core", "y", "xl", "z")
SHAPE = (2, 2, 4, 2, 4)
VMEM = pl.BlockSpec(memory_space=pltpu.VMEM)
SMEM = pl.BlockSpec(memory_space=pltpu.SMEM)
HBM = pl.BlockSpec(memory_space=pltpu.HBM)
MIB = 1 << 20
BF16 = jnp.bfloat16
F32 = jnp.float32
XH, CORE, Y, XL, Z = range(5)


def swap_table(xh=0, core=0, y=0, xl=0, z=0):
    by = (xh, core, y, xl, z)
    table = []
    for i in range(128):
        to = tuple(int(v) ^ w for v, w in zip(np.unravel_index(i, SHAPE), by))
        table.append((i, int(np.ravel_multi_index(to, SHAPE))))
    return table


def swap(x, **by):
    return lax.ppermute(x, AXES, swap_table(**by))


def dot_nt(u, v):
    return lax.dot_general(u, v, (((1,), (1,)), ((), ())), preferred_element_type=jnp.float32)


def call(body, shapes, inputs, places, name, out_place=None, scratch=(), limit=4, flops=0, size=MIB, **more):
    many = isinstance(shapes, list)
    shapes = shapes if many else [shapes]
    got = pl.pallas_call(
        body,
        out_shape=[jax.ShapeDtypeStruct(*v) for v in shapes],
        in_specs=places,
        out_specs=[out_place or VMEM] * len(shapes),
        scratch_shapes=list(scratch),
        compiler_params=pltpu.CompilerParams(vmem_limit_bytes=limit * MIB),
        cost_estimate=pl.CostEstimate(flops=flops, bytes_accessed=size, transcendentals=0),
        name=name,
        **more,
    )(*inputs)
    return got if many else got[0]


def split_kernel(at, left, mine, theirs):
    t = left[...].T
    upper, lower = t[:64], t[64:]
    mine[...] = jnp.where(at[XH] == 0, upper, lower)
    theirs[...] = jnp.where(at[XH] == 0, lower, upper)


def split(at, left):
    return call(split_kernel, [((64, 1280), BF16)] * 2, (at, left), [SMEM, VMEM], "split")


def cut_kernel(cuts, source, *refs):
    for cut, out in zip(cuts, refs[len(refs) - len(cuts):]):
        out[...] = source[cut]


def cut(source, cuts, after=()):
    shapes = [(tuple(len(range(n)[c]) for c, n in zip(cut, source.shape)), BF16) for cut in cuts]
    return call(functools.partial(cut_kernel, cuts), shapes, (source, *after), [VMEM] + [HBM] * len(after), "cut")


def stack_kernel(n, *refs):
    for i in range(n):
        refs[-1][i * 64:(i + 1) * 64, :] = refs[i][...]


def stack(pieces, after=()):
    n = len(pieces)
    shape = ((64 * n, pieces[0].shape[1]), BF16)
    return call(functools.partial(stack_kernel, n), shape, (*pieces, *after), [VMEM] * n + [HBM] * len(after), "stack")


def tile_kernel(j, at, *refs):
    la, lb, r = refs[0:5], refs[5:10], refs[10:15]
    keep, send, acc = refs[-3:]
    first = at[CORE] == 0
    lanes = slice(j * 128, (j + 1) * 128)
    place = ((0, 0, 4), (1, 0, 4), (3, 0, 4), (2, 0, 2), (2, 2, 2))
    for part in range(2):
        right = r[part][...]
        for k, (zr, start, count) in enumerate(place):
            out = jnp.dot(la[k][:, :1250], right, preferred_element_type=jnp.float32)
            for i in range(count):
                acc[part, start + i, at[Z] ^ zr] = out[i * 64:(i + 1) * 64]
    for part in range(2):
        right = jnp.concatenate([r[3][:, lanes], r[4][:, lanes]], axis=1) if part == 0 else r[2][...]
        for k, (yr, start, count) in enumerate(place):
            out = jnp.dot(lb[k][:, :1250], right, preferred_element_type=jnp.float32)
            for i in range(count):
                zs = at[Z] ^ (start + i)
                total = acc[part, yr, zs] + out[i * 64:(i + 1) * 64]
                rows = pl.ds(pl.multiple_of(yr * 256 + zs * 64, 64), 64)
                keep[part, rows, :] = jnp.where(first, total[:, :128], total[:, 128:])
                send[part, rows, :] = jnp.where(first, total[:, 128:], total[:, :128])


def tile(j, at, la, lb, r, after=()):
    return call(
        functools.partial(tile_kernel, j),
        [((2, 1024, 128), F32)] * 2,
        (at, *la, *lb, *r, *after),
        [SMEM] + [VMEM] * 15 + [HBM] * len(after),
        "tile",
        scratch=[pltpu.VMEM((2, 4, 4, 64, 256), F32)],
        limit=6,
        flops=2 * 1024 * 2500 * 512,
        size=10 * MIB,
    )


def turn_kernel(keep, got, own, other, total):
    lane = lax.broadcasted_iota(jnp.int32, (16, 128), 1)
    odd = (lane // 32) % 2 == 1
    high = lane // 64 == 1
    total[...] = keep[...] + got[...]
    for part, out in ((0, own), (1, other)):
        for group in range(16):
            v = []
            for c in range(4):
                rows = pl.ds(group * 4 + c, 16, stride=64)
                v.append(total[part, rows, :])
            w = [
                jnp.where(odd, pltpu.roll(v[1], 32, 1), v[0]),
                jnp.where(odd, v[1], pltpu.roll(v[0], 96, 1)),
                jnp.where(odd, pltpu.roll(v[3], 32, 1), v[2]),
                jnp.where(odd, v[3], pltpu.roll(v[2], 96, 1)),
            ]
            t = [
                jnp.where(high, pltpu.roll(w[2], 64, 1), w[0]),
                jnp.where(high, pltpu.roll(w[3], 64, 1), w[1]),
                jnp.where(high, w[2], pltpu.roll(w[0], 64, 1)),
                jnp.where(high, w[3], pltpu.roll(w[1], 64, 1)),
            ]
            for b in range(4):
                out[b * 16:(b + 1) * 16, group * 128:(group + 1) * 128] = t[b].astype(jnp.bfloat16)


def turn(keep, got):
    return call(turn_kernel, [((64, 2048), BF16)] * 2, (keep, got), [VMEM] * 2, "turn", scratch=[pltpu.VMEM((2, 1024, 128), F32)], size=3 * MIB)


def ladder_kernel(at, amp, part, *refs):
    halves, outs = refs[:-3], refs[-3:]
    for s, out in enumerate(outs):
        rows = pl.ds(pl.multiple_of((at[Z] ^ (s + 1)) * 256, 256), 256)
        total = dot_nt(amp[rows, :], part[...]).astype(BF16)
        if halves:
            out[:, :256] = halves[s][...]
            out[:, 256:] = total
        else:
            out[...] = total


def ladder(at, amp, part, halves=()):
    shape = (256, 512 if halves else 256)
    return call(
        ladder_kernel,
        [(shape, BF16)] * 3,
        (at, amp, part, *halves),
        [SMEM] + [VMEM] * (2 + len(halves)),
        "ladder",
        flops=2 * 768 * 2048 * 256,
        size=4 * MIB,
    )


def own_kernel(at, amp, mine, peer, *refs):
    rows = pl.ds(pl.multiple_of(at[Z] * 256, 256), 256)
    for k, part in enumerate((mine, peer)):
        refs[-1][:, k * 256:(k + 1) * 256] = dot_nt(amp[rows, :], part[...])


def own_ladder(at, amp, mine, peer, after):
    inputs = (at, amp, mine, peer, *after)
    places = [SMEM] + [VMEM] * 3 + [HBM] * len(after)
    return call(own_kernel, ((256, 512), F32), inputs, places, "own", flops=2 * 256 * 2048 * 512, size=4 * MIB)


def finish_kernel(j, own, r1, r2, r3, order, scale, *refs):
    out, held, sem = refs[-3:]
    total = own[...] + r1[...].astype(F32) + r2[...].astype(F32) + r3[...].astype(F32)
    turned = None
    for _ in range(3):
        term = total.astype(BF16)
        total = total - term.astype(F32)
        placed = jnp.dot(term, order[...], preferred_element_type=F32)
        turned = placed if turned is None else turned + placed
    lanes = pl.ds(j * 512, 512)
    held[...] = turned * scale[:, lanes]
    copy = pltpu.make_async_copy(held, out.at[:, lanes], sem)
    copy.start()
    copy.wait()


def finish(j, own, got, order, scale, out):
    before = [] if out is None else [out]
    return call(
        functools.partial(finish_kernel, j),
        ((256, 1024), F32),
        (own, *got, order, scale, *before),
        [VMEM] * 6 + [HBM] * len(before),
        "finish",
        out_place=HBM,
        scratch=[pltpu.VMEM((256, 512), F32), pltpu.SemaphoreType.DMA],
        flops=6 * 256 * 512 * 512,
        size=4 * MIB,
        input_output_aliases={6: 0} if before else {},
    )


def prepare_kernel(at, offsets, virt, pairs, occ, order, scale):
    s = lax.broadcasted_iota(jnp.int32, (512, 1), 0)
    pc, px, b, yr, zr = s // 256, (s // 64) % 4, (s // 16) % 4, (s // 4) % 4, s % 4
    xl, xh = at[XL] ^ (px % 2), at[XH] ^ (px // 2)
    target = (4 * (at[CORE] ^ pc) + b) * 64 + 16 * (at[Y] ^ yr) + 8 * xl + 2 * zr + xh
    columns = lax.broadcasted_iota(jnp.int32, (512, 512), 1)
    order[...] = jnp.where(columns == target, 1.0, 0.0).astype(BF16)

    lane = lax.broadcasted_iota(jnp.int32, (8, 128), 1)
    ea = jnp.zeros((8, 128), F32)
    for a in range(64):
        ea = jnp.where(lane % 64 == a, virt[offsets[0] + a], ea)
    b_start = offsets[1] + (at[Y] * 2 + at[XL]) * 16
    first, second = (jnp.broadcast_to(pairs[i:i + 1, :], (8, 256)).T[:, 0:1] for i in (0, 1))
    levels = lax.broadcasted_iota(jnp.int32, (256, 120), 1)
    occupied = jnp.sum(jnp.where(levels == first, occ[...], 0.0), axis=1, keepdims=True)
    occupied += jnp.sum(jnp.where(levels == second, occ[...], 0.0), axis=1, keepdims=True)
    weight = jnp.where(first == second, 0.5, 1.0)
    for b in range(0, 16, 2):
        eb = jnp.where(lane < 64, virt[b_start + b], virt[b_start + b + 1])
        scale[:, b * 64:(b + 2) * 64] = weight / ((eb + ea)[:1] - occupied)


def prepare(at, offsets, virt, pairs, occ):
    return call(
        prepare_kernel,
        [((512, 512), BF16), ((256, 1024), F32)],
        (at, offsets, virt, pairs.T, occ.reshape(1, -1)),
        [SMEM] * 3 + [VMEM] * 2,
        "prepare",
    )


def join_kernel(lanes, *refs):
    refs[-1][...] = jnp.concatenate([v[:, lanes] for v in refs[:-1]], axis=1)


def join(parts, lanes):
    shape = ((parts[0].shape[0], 128 * len(parts)), BF16)
    return call(functools.partial(join_kernel, lanes), shape, parts, [VMEM] * len(parts), "join")


def spread(x, axis, after):
    one, three = swap(x, **{axis: 1}), swap(x, **{axis: 3})
    (upper,), (lower,) = cut(one, [np.s_[:128, :]], after), cut(three, [np.s_[128:, :]], after)
    return [x, one, three, swap(upper, **{axis: 3}), swap(lower, **{axis: 1})]


def per_device(left, right, amplitudes, pair_list, offsets, occ_energy, virt_energy):
    at = jnp.stack([lax.axis_index(n) for n in AXES]).astype(jnp.int32)
    right = right.reshape(right.shape[0], 512)
    amp = amplitudes.reshape(1024, 2048)

    mine, theirs = split(at, jnp.pad(left, ((0, 30), (0, 0))))
    far = swap(theirs, xh=1)
    r0 = cut(right, [np.s_[:, :256]], (theirs,))
    mine = stack([mine], r0)
    far4 = [far] + [swap(far, z=s) for s in (1, 2, 3)]
    mine4 = [mine] + [swap(mine, y=s) for s in (1, 2, 3)]
    r0 += cut(right, [np.s_[:, 256:]], (mine4[1], mine4[3], far4[1], far4[3]))
    r1, r3 = [swap(v, xl=1) for v in r0], [swap(v, xl=1, xh=1) for v in r0]

    la = stack(mine4, (*far4[1:], r1[0], r3[0]))
    lb = stack(far4, (*mine4[1:], r1[0], r3[0]))
    la, lb = spread(la, "z", (r1[1], r3[1])), spread(lb, "y", (r1[1], r3[1]))
    r2 = swap(join(r1, np.s_[:128]), xl=1, xh=1), swap(join(r3, np.s_[128:]), xl=1)
    order, scale = prepare(at, offsets, virt_energy, pair_list, occ_energy)

    parts = []
    for j in range(CHUNKS):
        keep, send = tile(j, at, la, lb, (r0[j], r1[j], r3[j], *r2))
        own, other = turn(keep, swap(send, core=1))
        parts.append([own, swap(other, xl=1), swap(own, xh=1), swap(other, xl=1, xh=1)])
    out, after = None, (parts[1][1], parts[1][3])
    for j in range(CHUNKS):
        held = stack(parts[j], after)
        peer = swap(held, core=1)
        l1, l2, l3 = ladder(at, amp, peer, ladder(at, amp, held))
        l0 = own_ladder(at, amp, held, peer, (l1,))
        got = [swap(l1, z=1), swap(l3, z=3), swap(l2, z=2)]
        after = (got[0], got[1])
        out = finish(j, l0, got, order, scale, out)
    return out


def solution(mesh):
    mesh = jax.sharding.Mesh(mesh.devices.reshape(SHAPE), AXES)
    rows, cols = ("xh", "core"), ("y", "xl")
    placed = (
        P(rows, (*cols, "z")),
        P(rows, "z", cols),
        P(rows, "z", None),
        P((*rows, "z"), None),
        P(),
        P(),
        P(),
    )
    return jax.shard_map(
        per_device,
        mesh=mesh,
        in_specs=placed,
        out_specs=P((*rows, "z"), cols),
        check_vma=False,
    )
```
